32 devices in a mesh: tile: 8 (over z, x), rep: 4 (over y, core).
Axes of the slice: x: 2, y: 2, z: 4, core: 2. Of those that a mesh axis runs over, the one named last changes fastest.
Arguments:
- tokens: bfloat16 [2048, 108, 128], P(('tile', 'rep')), may hold values from -6 to 6
- absent: int32 [2048, 108], P(('tile', 'rep')), may hold values from 0 to 1, as said below
- send_counts: int32 [32, 8], P(('tile', 'rep')), may hold values from 0 to 8, as said below
- attn_gain: float32 [2, 128], replicated, may hold values from 0.25 to 1.75
- attn_shift: float32 [2, 128], replicated, may hold values from -3 to 3
- proj_qkv: bfloat16 [2, 128, 384], replicated, may hold values from -0.5 to 0.5
- proj_out: bfloat16 [2, 128, 128], replicated, may hold values from -2 to 2
- out_bias: float32 [2, 128], replicated, may hold values from -2.5 to 2.5
- feed_gain: float32 [2, 128], replicated, may hold values from 0.25 to 1.75
- feed_shift: float32 [2, 128], replicated, may hold values from -3 to 3
- proj_up: bfloat16 [2, 128, 512], replicated, may hold values from -0.5 to 0.5
- up_bias: float32 [2, 512], replicated, may hold values from -3 to 3
- proj_down: bfloat16 [2, 512, 128], replicated, may hold values from -0.25 to 0.25
- down_bias: float32 [2, 128], replicated, may hold values from -2.5 to 2.5
- cotangent: bfloat16 [2048, 108, 128], P(('tile', 'rep')), may hold values from -6 to 6
Outputs:
- output: bfloat16 [2048, 108, 128], P(('tile', 'rep'))
- grad_tokens: bfloat16 [2048, 108, 128], P(('tile', 'rep'))
- grad_attn_gain: float32 [2, 128], replicated
- grad_attn_shift: float32 [2, 128], replicated
- grad_proj_qkv: float32 [2, 128, 384], replicated
- grad_proj_out: float32 [2, 128, 128], replicated
- grad_out_bias: float32 [2, 128], replicated
- grad_feed_gain: float32 [2, 128], replicated
- grad_feed_shift: float32 [2, 128], replicated
- grad_proj_up: float32 [2, 128, 512], replicated
- grad_up_bias: float32 [2, 512], replicated
- grad_proj_down: float32 [2, 512, 128], replicated
- grad_down_bias: float32 [2, 128], replicated
The draws below stay inside these ranges and needn't reach their ends.
Inputs may be any that keep to these rules, and one draw needn't show every extreme that they name: 1 marks an absent token; every pixel series has at least one present token. `send_counts`: each entry is at most 8, reached in every draw; row d sends its slots in order, its first entry's pixels first; within one index of rep, the senders give one receiver at most 32 pixels in all, and some receiver gets exactly 32 in every draw.
All inputs are finite; a program needn't handle non-finite values.
Results may differ from the reference program's by a relative error of at most 0.014.
Values may be sent and summed in bfloat16 or wider, within the bound.
No kernel may reach another device: no remote copies, remote signals or barrier semaphores. Data moves between devices by JAX's collectives and lax.ppermute only.
A program may use at most 192 MiB of HBM per device.

```python
import jax
import jax.numpy as jnp
from jax import lax

D = 128
FF = 512
HEADS = 8
HEAD_DIM = 16
L = 108
LAYERS = 2
PIX_DEV = 64
SLOT = 8
RECV = 32
PIXELS = 2048
N_TILE = 8
N_REP = 4


def draw_absent(key, part):
    key = jax.random.fold_in(key, 5)
    first, second = jax.random.split(key)
    rolls = jax.random.randint(first, (PIXELS, L), 0, 10)
    kept = jax.random.randint(second, (PIXELS, 1), 0, L)
    position = lax.broadcasted_iota(jnp.int32, (PIXELS, L), 1)
    return jnp.where((rolls < 3) & (position != kept), 1, 0).astype(jnp.int32)


def draw_send_counts(key, part):
    key = jax.random.fold_in(key, 11)
    first, second, third = jax.random.split(key, 3)
    level = jax.random.randint(first, (N_TILE, N_REP, 1), 1, 4)
    rolls = jax.random.randint(second, (N_TILE, N_REP, N_TILE), 0, SLOT + 1)
    counts = jnp.minimum(SLOT, rolls * level // 2)
    filled = jax.random.randint(third, (1, N_REP, 1), 0, N_TILE)
    column = lax.broadcasted_iota(jnp.int32, (N_TILE, N_REP, N_TILE), 2)
    counts = jnp.where(column == filled, SLOT, counts)
    before = jnp.cumsum(counts, axis=0) - counts
    capped = jnp.minimum(counts, jnp.maximum(RECV - before, 0))
    return capped.reshape(N_TILE * N_REP, N_TILE).astype(jnp.int32)


def block_scale(rng, shape, pieces, least, top_value):
    def one(dim, shards_of):
        draws = jax.random.uniform(jax.random.fold_in(jax.random.fold_in(rng, 6), dim), (shards_of,), jnp.float32, least / len(pieces), top_value / len(pieces))
        return jnp.repeat(jnp.exp(draws), shape[dim] // shards_of).reshape((-1,) + (1,) * (len(shape) - dim - 1))

    factor_of = one(*pieces[0])
    for cut in pieces[1:]:
        factor_of = factor_of * one(*cut)
    return factor_of


def gaussian(rng, shape, scale, limit, cuts=(), held_as=jnp.bfloat16):
    loudness = block_scale(rng, shape, cuts, -0.22, 0.18) if cuts else 1.0
    values = jax.random.normal(rng, shape, jnp.float32) * scale * loudness
    return jnp.minimum(jnp.maximum(values, -limit), limit).astype(held_as)


def setup_inputs(seed: int = 0) -> dict:
    streams_of = jax.random.split(jax.random.key(seed), 16)
    tokens = gaussian(streams_of[0], (PIXELS, L, D), 1.0, 6.0, ((0, 32),))
    absent = draw_absent(jax.random.fold_in(streams_of[15], 71), 0)
    send_counts = draw_send_counts(jax.random.fold_in(streams_of[15], 71), 0)
    attn_gain = jnp.clip(1.0 + 0.15 * jax.random.normal(streams_of[3], (LAYERS, D), jnp.float32), 0.25, 1.75)
    attn_shift = gaussian(streams_of[4], (LAYERS, D), 0.5, 3.0, (), jnp.float32)
    proj_qkv = gaussian(streams_of[5], (LAYERS, D, 3 * D), D ** -0.5, 0.5)
    proj_out = gaussian(streams_of[6], (LAYERS, D, D), 8 ** -0.5, 2.0)
    out_bias = gaussian(streams_of[7], (LAYERS, D), 0.4, 2.5, (), jnp.float32)
    feed_gain = jnp.clip(1.0 + 0.15 * jax.random.normal(streams_of[8], (LAYERS, D), jnp.float32), 0.25, 1.75)
    feed_shift = gaussian(streams_of[9], (LAYERS, D), 0.5, 3.0, (), jnp.float32)
    proj_up = gaussian(streams_of[10], (LAYERS, D, FF), D ** -0.5, 0.5)
    up_bias = gaussian(streams_of[11], (LAYERS, FF), 0.5, 3.0, (), jnp.float32)
    proj_down = gaussian(streams_of[12], (LAYERS, FF, D), FF ** -0.5, 0.25)
    down_bias = gaussian(streams_of[13], (LAYERS, D), 0.4, 2.5, (), jnp.float32)
    cotangent = gaussian(streams_of[14], (PIXELS, L, D), 1.0, 6.0, ((0, 32),))
    return {"tokens": tokens, "absent": absent, "send_counts": send_counts, "attn_gain": attn_gain, "attn_shift": attn_shift, "proj_qkv": proj_qkv, "proj_out": proj_out, "out_bias": out_bias, "feed_gain": feed_gain, "feed_shift": feed_shift, "proj_up": proj_up, "up_bias": up_bias, "proj_down": proj_down, "down_bias": down_bias, "cotangent": cotangent}


@jax.custom_vjp
def low(v):
    return lax.optimization_barrier(v.astype(jnp.bfloat16)).astype(jnp.float32)

@jax.custom_vjp
def low_back(v):
    return v

def low_keep(v):
    return (low(v), None)

def low_pass(kept, grad):
    return (grad,)

def back_keep(v):
    return (v, None)

def back_low(kept, grad):
    return (low(grad),)
low.defvjp(low_keep, low_pass)
low_back.defvjp(back_keep, back_low)
highest = lax.Precision.HIGHEST

def layer_norm(values, gain, shift):
    center = values - lax.optimization_barrier(jnp.mean(values, axis=-1, keepdims=True))
    spread = lax.optimization_barrier(jnp.mean(center * center, axis=-1, keepdims=True))
    return center * lax.rsqrt(spread + 1e-05) * gain + shift

def one_layer(state, absentb, weights):
    a_gain, a_shift, w_qkv, w_out, b_out, f_gain, f_shift, w_up, b_up, w_down, b_down = weights
    count, length, width = state.shape
    normed = low(layer_norm(state, a_gain, a_shift))
    packed = low(low_back(jnp.einsum('pld,de->ple', normed, w_qkv, precision=highest)))
    queries = packed[..., :width].reshape(count, length, HEADS, HEAD_DIM)
    keys = packed[..., width:2 * width].reshape(count, length, HEADS, HEAD_DIM)
    values = packed[..., 2 * width:].reshape(count, length, HEADS, HEAD_DIM)
    raw = jnp.einsum('plhd,pmhd->phlm', queries, keys, precision=highest) / jnp.sqrt(jnp.float32(HEAD_DIM))
    scores = low_back(jnp.where(absentb[:, None, None, :] == 1, -1000000000.0, raw))
    probs = low(jax.nn.softmax(scores, axis=-1))
    mixed = low(low_back(jnp.einsum('phlm,pmhd->plhd', probs, values, precision=highest)))
    mixed = mixed.reshape(count, length, width)
    after = state + low_back(jnp.einsum('pld,de->ple', mixed, w_out, precision=highest)) + b_out
    normed_two = low(layer_norm(after, f_gain, f_shift))
    hidden = low_back(jnp.einsum('pld,df->plf', normed_two, w_up, precision=highest)) + b_up
    active = low(jax.nn.gelu(hidden, approximate=False))
    return after + low_back(jnp.einsum('plf,fd->pld', active, w_down, precision=highest)) + b_down

def two_layers(state, absentb, params):
    for layer in range(LAYERS):
        state = one_layer(state, absentb, tuple((item[layer] for item in params)))
    return state

def reference(tokens, absent, send_counts, attn_gain, attn_shift, proj_qkv, proj_out, out_bias, feed_gain, feed_shift, proj_up, up_bias, proj_down, down_bias, cotangent):
    totals = lax.optimization_barrier(jnp.sum(send_counts, axis=1))
    slots = jnp.arange(PIX_DEV, dtype=jnp.int32)
    live = (slots[None, :] < totals[:, None]).reshape(-1).astype(jnp.float32)
    params = tuple((item.astype(jnp.float32) for item in (attn_gain, attn_shift, proj_qkv, proj_out, out_bias, feed_gain, feed_shift, proj_up, up_bias, proj_down, down_bias)))
    count = tokens.shape[0]
    groups = count // 32
    absent_groups = absent.reshape(groups, 32, L)

    def forward(state, weights):
        blocks = state.reshape(groups, 32, L, D)
        step = jax.checkpoint(two_layers)
        result = lax.map(lambda pair: step(pair[0], pair[1], weights), (blocks, absent_groups))
        return result.reshape(state.shape) * live[:, None, None]
    result, backward = jax.vjp(forward, tokens.astype(jnp.float32), params)
    grad_state, grad_params = backward(cotangent.astype(jnp.float32))
    return (result.astype(jnp.bfloat16), grad_state.astype(jnp.bfloat16), grad_params[0], grad_params[1], grad_params[2], grad_params[3], grad_params[4], grad_params[5], grad_params[6], grad_params[7], grad_params[8], grad_params[9], grad_params[10])
```

```python
import functools

import jax
import jax.numpy as jnp
from jax import lax
from jax.experimental import pallas as pl
from jax.experimental.pallas import tpu as pltpu
from jax.sharding import PartitionSpec as P

HEADS = 8
HEAD_DIM = 16
STEP = 16
BLOCK = CHUNK = 4
PACK = 1552
LOG2E = 1.4426950408889634
F32 = jnp.float32
BF16 = jnp.bfloat16


def dot_nn(left, right):
    return lax.dot_general(left, right, (((1,), (0,)), ((), ())), preferred_element_type=F32)


def dot_nt(left, right):
    return lax.dot_general(left, right, (((1,), (1,)), ((), ())), preferred_element_type=F32)


def dot_tn(left, right):
    return lax.dot_general(left, right, (((0,), (0,)), ((), ())), preferred_element_type=F32)


def gelu_parts(u):
    phi = lax.erf(u * 0.7071067811865476) + 1.0
    x = u * 0.8493218002880191
    e = jnp.exp2(-0.32574806473615 - x * x)
    return u * phi, phi + u * e


def norm_parts(x):
    mean = jnp.sum(x, axis=-1, keepdims=True) * (1.0 / 128)
    center = x - mean
    spread = jnp.sum(center * center, axis=-1, keepdims=True) * (1.0 / 128)
    r = lax.rsqrt(spread + 1e-05)
    return center * r, jnp.broadcast_to(r, x.shape)


def norm_back(dh, n, r, gain):
    e = dh * gain
    m1 = jnp.sum(e, axis=-1, keepdims=True) * (1.0 / 128)
    m2 = jnp.sum(e * n, axis=-1, keepdims=True) * (1.0 / 128)
    return r * (e - m1 - n * m2)


def fold_rows(v):
    rows, width = v.shape
    return jnp.sum(v.reshape(rows // 8, 8, width), axis=0)


def body(
    counts_ref,
    me_ref,
    tok_ref,
    cot_ref,
    absent_ref,
    a_gain,
    a_shift,
    w_qkv,
    w_out,
    b_out,
    f_gain,
    f_shift,
    w_up,
    b_up,
    w_down,
    b_down,
    out_ref,
    gtok_ref,
    keep_ref,
    send_ref,
    g_qkv,
    g_out,
    g_up,
    stage,
    xs,
    xm,
    n1,
    n2,
    r1,
    r2,
    h1,
    h2,
    qkv,
    prob,
    ot,
    act,
    slope,
    dz,
    dy,
    du,
    dqkv,
    inv_tot,
    half_down,
    mask,
    g_buf,
    acc_down,
    acc_vec,
    acc_bup,
    tin,
    cin,
    *bufs,
    peers,
    length,
):
    ds_bufs = bufs
    step = pl.program_id(0)
    steps = pl.num_programs(0)
    total = counts_ref[0, 0]
    for peer in range(1, peers):
        total = total + counts_ref[0, peer]
    first = step * STEP
    rows = CHUNK * 112

    @pl.when(step == 0)
    def _():
        for ref in (stage, g_buf, g_qkv, g_out, g_up, acc_down, acc_vec, acc_bup, xs, qkv, dz):
            ref[...] = jnp.zeros_like(ref)
        mask[...] = jnp.full_like(mask, -1e9)
        mask[:, :length] = jnp.where(absent_ref[...] == 1, -1e9, 0.0)
        half_down[...] = w_down[...] * 0.5
        qkv[:, :, :, 512:640] = jnp.ones((2, BLOCK, 128, 128), BF16)

    def fwd_qkv(layer, chunk):
        at = pl.ds(chunk * CHUNK, CHUNK)
        x = xs[at].reshape(rows, 128)
        n, r = norm_parts(x)
        n1[layer, at] = n.reshape(CHUNK, 112, 128)
        r1[layer, at] = r.reshape(CHUNK, 112, 128)
        h = (n * a_gain[layer : layer + 1] + a_shift[layer : layer + 1]).astype(BF16)
        h1[layer, at] = h.reshape(CHUNK, 112, 128)
        packed = dot_nn(h, w_qkv[layer])
        q = (packed[:, 0:128] * (0.25 * LOG2E)).astype(BF16)
        k = packed[:, 128:256].astype(BF16)
        v = packed[:, 256:384].astype(BF16)
        qkv[layer, at, 0:112, 0:128] = q.reshape(CHUNK, 112, 128)
        qkv[layer, at, 0:112, 128:256] = k.reshape(CHUNK, 112, 128)
        qkv[layer, at, 0:112, 384:512] = v.reshape(CHUNK, 112, 128)

    def pair_rows(rows, pair):
        zero = jnp.zeros((16, 128), BF16)
        one = rows[32 * pair : 32 * pair + 16]
        two = rows[32 * pair + 16 : 32 * pair + 32]
        return jnp.concatenate(
            [jnp.concatenate([one, zero], axis=1), jnp.concatenate([zero, two], axis=1)], axis=0
        )

    def parity(rows):
        zero = jnp.zeros((16, 128), BF16)
        tiles = [rows[16 * h : 16 * h + 16] for h in range(HEADS)]
        even = [tile if h % 2 == 0 else zero for h, tile in enumerate(tiles)]
        odd = [tile if h % 2 == 1 else zero for h, tile in enumerate(tiles)]
        return jnp.concatenate(
            [jnp.concatenate(even, axis=0), jnp.concatenate(odd, axis=0)], axis=1
        )

    def one_pair(pair):
        lane = lax.broadcasted_iota(jnp.int32, (1, 128), 1)
        return jnp.where((lane >= 32 * pair) & (lane < 32 * pair + 32), 1.0, 0.0).astype(BF16)

    def staged(items, stages):
        for tick in range(len(items) + len(stages) - 1):
            for lag, stage in enumerate(stages):
                if 0 <= tick - lag < len(items):
                    stage(tick - lag, *items[tick - lag])

    def fwd_attend(layer, chunk):
        base = chunk * CHUNK
        first_row = jnp.where(lax.broadcasted_iota(jnp.int32, (16, 256), 0) == 0, 1.0, 0.0)
        first_row = first_row.astype(BF16)
        sum_row = jnp.ones((16, 112), BF16)
        pairs = [one_pair(j) for j in range(4)]
        queries, values = {}, {}

        def prepare(i, key):
            qt = qkv[layer, base + i, :, 0:128].T
            queries[key] = jnp.concatenate([parity(qt), first_row], axis=0)
            values[key] = qkv[layer, base + i, :, 384:512].T

        def scores(i, key):
            k = qkv[layer, base + i, 0:112, 128:256]
            k = jnp.concatenate([k * pairs[j] for j in range(4)], axis=0)
            m = qkv[layer, base + i, 0:112, 256:272]
            k = jnp.concatenate([k, jnp.concatenate([m] * 4, axis=0)], axis=1)
            return dot_nn(k, queries[key])

        def weigh(i, j, part):
            prob[layer, base + i, :, 256 * j : 256 * j + 256] = jnp.exp2(part).astype(BF16)

        def mix(i, j, key):
            pr = prob[layer, base + i, :, 256 * j : 256 * j + 256]
            left = jnp.concatenate([values[key][32 * j : 32 * j + 32, 0:112], sum_row], axis=0)
            o = dot_nn(left, pr)
            inv = 1.0 / o[32:33]
            one = o[0:16, 0:128] * inv[:, 0:128]
            two = o[16:32, 128:256] * inv[:, 128:256]
            ot[layer, base + i, 32 * j : 32 * j + 32, :] = jnp.concatenate(
                [one, two], axis=0
            ).astype(BF16)
            inv_tot[layer, base + i, 2 * j : 2 * j + 1] = inv[:, 0:128]
            inv_tot[layer, base + i, 2 * j + 1 : 2 * j + 2] = inv[:, 128:256]
            return o[32:33]

        def run_scores(i):
            s = scores(i, i)
            for j in range(4):
                weigh(i, j, s[112 * j : 112 * j + 112])

        most, least = [], []

        def run_mix(i):
            for j in range(4):
                tot = mix(i, j, i)
                most.append(tot)

        for i in range(CHUNK):
            prepare(i, i)
        for i in range(CHUNK):
            run_scores(i)
        for i in range(CHUNK):
            run_mix(i)
        high, low = most[0], most[0]
        for tot in most[1:]:
            high, low = jnp.maximum(high, tot), jnp.minimum(low, tot)
        good = (jnp.max(high) <= 2.0**100) & (jnp.min(low) >= 2.0**-100)

        @pl.when(jnp.logical_not(good))
        def _():
            def again(i):
                prepare(i, -1)
                s = scores(i, -1)
                for j in range(4):
                    part = s[112 * j : 112 * j + 112]
                    weigh(i, j, part - jnp.max(part, axis=0, keepdims=True))
                for j in range(4):
                    mix(i, j, -1)

            loop(CHUNK, again)

    def fwd_feed(layer, chunk):
        at = pl.ds(chunk * CHUNK, CHUNK)
        for i in range(CHUNK):
            p = chunk * CHUNK + i
            z = dot_tn(ot[layer, p], w_out[layer])[0:112]
            x = xs[p] + z + b_out[layer : layer + 1]
            n, r = norm_parts(x)
            n2[layer, p] = n
            r2[layer, p] = r
            xm[p] = x + b_down[layer : layer + 1]
            h = (n * f_gain[layer : layer + 1] + f_shift[layer : layer + 1]).astype(BF16)
            h2[layer, p] = h
        h = h2[layer, at].reshape(rows, 128)
        for j in range(2):
            cols = slice(256 * j, 256 * j + 256)
            u = dot_nn(h, w_up[layer, :, cols])
            for lo in range(0, rows, 16):
                a, s = gelu_parts(u[lo : lo + 16] + b_up[layer : layer + 1, cols])
                p, q = chunk * CHUNK + lo // 112, lo % 112
                act[layer, p, q : q + 16, cols] = a.astype(BF16)
                slope[layer, p, q : q + 16, cols] = s.astype(BF16)
        y = dot_nn(act[layer, at].reshape(rows, 512), half_down[layer])
        xs[at] = xm[at] + y.reshape(CHUNK, 112, 128)

    def back_feed(layer, chunk):
        at = pl.ds(chunk * CHUNK, CHUNK)
        dx = xs[at].reshape(rows, 128)
        dyl = dx.astype(BF16)
        dy[at] = dyl.reshape(CHUNK, 112, 128)
        acc_vec[layer, 5] += fold_rows(dx)
        for j in range(2):
            cols = slice(256 * j, 256 * j + 256)
            d = dot_nt(dyl, half_down[layer, cols, :])
            total = jnp.zeros((8, 256), F32)
            for lo in range(0, rows, 16):
                p, q = chunk * CHUNK + lo // 112, lo % 112
                part = d[lo : lo + 16] * slope[layer, p, q : q + 16, cols].astype(F32)
                du[p, q : q + 16, cols] = part.astype(BF16)
                total = total + part[0:8] + part[8:16]
            acc_bup[layer, :, cols] += total
        dh_all = dot_nt(du[at].reshape(rows, 512), w_up[layer])
        totals = [jnp.zeros((8, 128), F32) for _ in range(3)]
        for i in range(CHUNK):
            p = chunk * CHUNK + i
            dh = dh_all[112 * i : 112 * i + 112]
            n = n2[layer, p]
            dxm = xs[p] + norm_back(dh, n, r2[layer, p], f_gain[layer : layer + 1])
            xm[p] = dxm
            dz[p, 0:112] = dxm.astype(BF16)
            totals[0] = totals[0] + fold_rows(dxm)
            totals[1] = totals[1] + fold_rows(dh * n)
            totals[2] = totals[2] + fold_rows(dh)
        for item in range(3):
            acc_vec[layer, 2 + item] += totals[item]

    def grads_feed(layer):
        flat = BLOCK * 112
        g_up[layer] += dot_tn(h2[layer].reshape(flat, 128), du[...].reshape(flat, 512))
        acc_down[layer] += dot_tn(dy[...].reshape(flat, 128), act[layer].reshape(flat, 512))

    def back_attend(layer, chunk):
        base = chunk * CHUNK
        pairs = [one_pair(j) for j in range(4)]
        which = lax.broadcasted_iota(jnp.int32, (16, 256), 0)
        side = lax.broadcasted_iota(jnp.int32, (112, 16), 1)
        picks = [
            jnp.where((side == 2 * j) | (side == 2 * j + 1), 1.0, 0.0).astype(BF16)
            for j in range(4)
        ]
        head = lax.broadcasted_iota(jnp.int32, (16, 128), 1) // 16
        row = lax.broadcasted_iota(jnp.int32, (16, 128), 0)
        head_sums = [
            jnp.where((row < 8) & (head == row // 2 * 2 + odd), -1.0, 0.0).astype(BF16)
            for odd in range(2)
        ]
        queries, keys, grads, whole = {}, {}, {}, {}

        def prepare(at, i, pair):
            if pair:
                return
            p = base + i
            queries[i] = qkv[layer, p, :, 0:128].T
            keys[i] = qkv[layer, p, :, 128:256].T
            full = dot_nt(w_out[layer], dz[p])
            scaled = jnp.concatenate(
                [
                    full[16 * h : 16 * h + 16] * inv_tot[layer, p, h : h + 1]
                    for h in range(HEADS)
                ],
                axis=0,
            )
            prod = (scaled * ot[layer, p].astype(F32)).astype(BF16)
            d = jnp.concatenate([dot_nn(head_sums[0], prod), dot_nn(head_sums[1], prod)], axis=1)
            high = d.astype(BF16).astype(F32)
            last = jnp.where(which % 2 == 0, high, d - high)
            dobt = scaled.astype(BF16)
            grads[i] = dobt
            whole[i] = jnp.concatenate([parity(dobt), last.astype(BF16)], axis=0)

        def prods(at, i, pair):
            if pair:
                return
            v = qkv[layer, base + i, 0:112, 384:512]
            v = jnp.concatenate([v * pairs[j] for j in range(4)], axis=0)
            v = jnp.concatenate([v, jnp.concatenate(picks, axis=0)], axis=1)
            dp = dot_nn(v, whole[i]).astype(BF16)
            for j in range(4):
                pr = prob[layer, base + i, :, 256 * j : 256 * j + 256]
                ds_bufs[4 * i + j][...] = pr * dp[112 * j : 112 * j + 112]

        def finish(at, i, pair):
            pr = prob[layer, base + i, :, 256 * pair : 256 * pair + 256]
            ds = ds_bufs[at][...]
            here = slice(32 * pair, 32 * pair + 32)
            g_buf[i, 2, here, 0:112] = dot_nt(pair_rows(grads[i], pair), pr).astype(BF16)
            dk = dot_nt(pair_rows(queries[i], pair), ds) * (1.0 / LOG2E)
            g_buf[i, 1, here, 0:112] = dk.astype(BF16)
            dq = dot_nn(keys[i][here, 0:112], ds)
            dq = jnp.concatenate([dq[0:16, 0:128], dq[16:32, 128:256]], axis=0) * 0.25
            g_buf[i, 0, here, :] = dq.astype(BF16)

        def turn(at, i, pair):
            if pair == 3:
                for j in range(3):
                    dqkv[base + i, :, 128 * j : 128 * j + 128] = g_buf[i, j].T[0:112]

        items = [(i, pair) for i in range(CHUNK) for pair in range(4)]
        for stage in (prepare, prods, finish, turn):
            for at, item in enumerate(items):
                stage(at, *item)
        add = jnp.zeros((128, 128), F32)
        for i in range(0, CHUNK, 2):
            left = jnp.concatenate([ot[layer, base + i], ot[layer, base + i + 1]], axis=1)
            add = add + dot_nn(left, dz[pl.ds(base + i, 2)].reshape(256, 128))
        g_out[layer] += add

    def back_qkv(layer, chunk):
        at = pl.ds(chunk * CHUNK, CHUNK)
        d = dqkv[at].reshape(rows, 384)
        dh = dot_nt(d, w_qkv[layer])
        n = n1[layer, at].reshape(rows, 128)
        r = r1[layer, at].reshape(rows, 128)
        dx = xm[at].reshape(rows, 128) + norm_back(dh, n, r, a_gain[layer : layer + 1])
        xs[at] = dx.reshape(CHUNK, 112, 128)
        acc_vec[layer, 0] += fold_rows(dh * n)
        acc_vec[layer, 1] += fold_rows(dh)

    def grads_qkv(layer):
        flat = BLOCK * 112
        g_qkv[layer] += dot_tn(h1[layer].reshape(flat, 128), dqkv[...].reshape(flat, 384))

    def loop(count, func):
        def one(i, carry):
            func(i)
            return carry

        lax.fori_loop(0, count, one, 0)

    @pl.when(first < total)
    def _():
        cin[...] = cot_ref[...].astype(F32).reshape(length * STEP, 128)
        tin[...] = tok_ref[...].astype(F32).reshape(length * STEP, 128)

        def group(g):
            lane = lax.broadcasted_iota(jnp.int32, (128, 128), 1)
            for i in range(BLOCK):
                p = g * BLOCK + i
                xs[i, 0:length, :] = tin[pl.ds(p, length, stride=STEP), :]
                xs[i, length:112, :] = jnp.zeros((112 - length, 128), F32)
                row = jnp.broadcast_to(mask[pl.ds(first + p, 1), :], (128, 128)).T
                row = jnp.where(lane == 0, row, 0.0).astype(BF16)[0:112]
                for layer in (0, 1):
                    qkv[layer, i, 0:112, 256:384] = row
            for layer in (0, 1):
                fwd_qkv(layer, 0)
                fwd_attend(layer, 0)
                fwd_feed(layer, 0)
            for i in range(BLOCK):
                p = g * BLOCK + i
                live = first + p < total
                tin[pl.ds(p, length, stride=STEP), :] = jnp.where(live, xs[i, 0:length, :], 0.0)
                xs[i, 0:length, :] = jnp.where(live, cin[pl.ds(p, length, stride=STEP), :], 0.0)
                xs[i, length:112, :] = jnp.zeros((112 - length, 128), F32)
            for layer in (1, 0):
                back_feed(layer, 0)
                grads_feed(layer)
                back_attend(layer, 0)
                back_qkv(layer, 0)
                grads_qkv(layer)
            for i in range(BLOCK):
                cin[pl.ds(g * BLOCK + i, length, stride=STEP), :] = xs[i, 0:length, :]

        groups = jnp.minimum((total - first + BLOCK - 1) // BLOCK, STEP // BLOCK)
        loop(groups, group)

        def clear(g):
            for i in range(BLOCK):
                zero = jnp.zeros((length, 128), F32)
                tin[pl.ds(g * BLOCK + i, length, stride=STEP), :] = zero
                cin[pl.ds(g * BLOCK + i, length, stride=STEP), :] = zero

        lax.fori_loop(groups, STEP // BLOCK, lambda g, c: (clear(g), c)[1], 0)
        out_ref[...] = tin[...].reshape(length, STEP, 128).astype(BF16)
        gtok_ref[...] = cin[...].reshape(length, STEP, 128).astype(BF16)

    @pl.when(first >= total)
    def _():
        out_ref[...] = jnp.zeros_like(out_ref)
        gtok_ref[...] = jnp.zeros_like(gtok_ref)

    @pl.when(step == steps - 1)
    def _():
        for layer in (0, 1):
            base = PACK * layer
            for j in range(3):
                stage[base + 128 * j : base + 128 * j + 128] = g_qkv[
                    layer, :, 128 * j : 128 * j + 128
                ]
            stage[base + 384 : base + 512] = g_out[layer]
            for j in range(4):
                cols = slice(128 * j, 128 * j + 128)
                stage[base + 512 + 128 * j : base + 640 + 128 * j] = g_up[layer, :, cols]
                stage[base + 1024 + 128 * j : base + 1152 + 128 * j] = (
                    acc_down[layer, :, cols].T * 0.5
                )
            small = [jnp.sum(acc_vec[layer, item], axis=0, keepdims=True) for item in range(6)]
            bup = jnp.sum(acc_bup[layer], axis=0, keepdims=True)
            small += [bup[:, 128 * j : 128 * j + 128] for j in range(4)]
            small.append(jnp.zeros((6, 128), F32))
            stage[base + 1536 : base + PACK] = jnp.concatenate(small, axis=0)
        chunks, rows_each, _ = keep_ref.shape

        def put(at, carry):
            for half, ref in ((0, keep_ref), (1, send_ref)):
                to = me_ref[0] ^ offset_of(at, half, 2 * chunks)
                ref[at] = stage[pl.ds(pl.multiple_of(to * rows_each, 8), rows_each)].astype(BF16)
            return carry

        lax.fori_loop(0, chunks, put, 0)


def reduce_stages(devices):
    bits = devices.bit_length() - 1
    stages, at = [[0]], 1
    while at < bits:
        stages.append(list(range(at, min(at + 2, bits))))
        at += 2
    return stages


def offset_of(at, half, devices):
    offset, left = half, devices.bit_length() - 2
    for bits in reduce_stages(devices)[1:]:
        left -= len(bits)
        offset = offset | (((at >> left) & (2 ** len(bits) - 1)) << bits[0])
    return offset


def partner(x, offset, sizes):
    pairs = [(i, i ^ offset) for i in range(sizes[0] * sizes[1])]
    return lax.ppermute(x, ("tile", "rep"), pairs)


def add_split_body(*refs, parts, ways):
    total = refs[0][...].astype(F32)
    for ref in refs[1:parts]:
        total = total + ref[...].astype(F32)
    low = total.astype(BF16)
    each = low.shape[0] // ways
    for k in range(ways):
        refs[parts + k][...] = low[each * k : each * k + each]


def add_split(pieces, ways):
    count = pieces[0].shape[0]
    shape = (count // ways,) + pieces[0].shape[1:]
    return pl.pallas_call(
        functools.partial(add_split_body, parts=len(pieces), ways=ways),
        out_shape=[jax.ShapeDtypeStruct(shape, BF16)] * ways,
        name="add_split",
    )(*pieces)


def join_body(*refs):
    count = refs[0].shape[0]
    for k, ref in enumerate(refs[:-1]):
        refs[-1][count * k : count * k + count] = ref[...]


def join(pieces):
    shape = (pieces[0].shape[0] * len(pieces),) + pieces[0].shape[1:]
    return pl.pallas_call(
        join_body, out_shape=jax.ShapeDtypeStruct(shape, BF16), name="join"
    )(*pieces)


def reduce_all(keep, send, sizes):
    stages = reduce_stages(sizes[0] * sizes[1])
    pieces = [keep, partner(send, 1, sizes)]
    for bits in stages[1:]:
        parts = add_split(pieces, 2 ** len(bits))
        pieces = [parts[0]] + [
            partner(parts[k], k << bits[0], sizes) for k in range(1, len(parts))
        ]
    (own,) = add_split(pieces, 1)
    for bits in reversed(stages[1:]):
        own = join(
            [own] + [partner(own, k << bits[0], sizes) for k in range(1, 2 ** len(bits))]
        )
    return own, partner(own, 1, sizes)


def unpack_body(me_ref, *refs, chunks):
    pieces, outs, stage = refs[:2], refs[2:-1], refs[-1]
    g_ag, g_as, g_qkv, g_out, g_ob, g_fg, g_fs, g_up, g_bup, g_down, g_db = outs
    each = pieces[0].shape[1]

    def put(at, carry):
        for half, ref in enumerate(pieces):
            to = me_ref[0] ^ offset_of(at, half, chunks)
            stage[pl.ds(pl.multiple_of(to * each, 8), each)] = ref[at].astype(F32)
        return carry

    lax.fori_loop(0, chunks // 2, put, 0)
    for layer in (0, 1):
        base = PACK * layer
        for j in range(3):
            g_qkv[layer, :, 128 * j : 128 * j + 128] = stage[
                base + 128 * j : base + 128 * j + 128
            ]
        g_out[layer] = stage[base + 384 : base + 512]
        for j in range(4):
            cols = slice(128 * j, 128 * j + 128)
            g_up[layer, :, cols] = stage[base + 512 + 128 * j : base + 640 + 128 * j]
            g_bup[layer : layer + 1, cols] = stage[base + 1542 + j : base + 1543 + j]
        g_down[layer] = stage[base + 1024 : base + 1536]
        for item, ref in enumerate((g_ag, g_as, g_ob, g_fg, g_fs, g_db)):
            ref[layer : layer + 1] = stage[base + 1536 + item : base + 1537 + item]


def unpack(me, own, other, params):
    chunks = own.shape[0] * 2
    whole = pl.BlockSpec(memory_space=pltpu.VMEM)
    return pl.pallas_call(
        functools.partial(unpack_body, chunks=chunks),
        in_specs=[pl.BlockSpec(memory_space=pltpu.SMEM), whole, whole],
        out_specs=[whole] * len(params),
        out_shape=[jax.ShapeDtypeStruct(item.shape, F32) for item in params],
        scratch_shapes=[pltpu.VMEM((chunks * own.shape[1], 128), F32)],
        compiler_params=pltpu.CompilerParams(vmem_limit_bytes=32 << 20),
        name="unpack",
    )(me, own, other)


def layers(counts, me, tokens, cotangent, absent, weights, chunks, each):
    length, pixels, width = tokens.shape
    peers = counts.shape[1]
    count = weights[0].shape[0]

    def live_block(i, counts_ref, me_ref):
        total = counts_ref[0, 0]
        for peer in range(1, peers):
            total = total + counts_ref[0, peer]
        last = jnp.maximum((total + STEP - 1) // STEP - 1, 0)
        return (0, jnp.minimum(i, last), 0)

    def whole(shape):
        return pl.BlockSpec(shape, lambda i, c, m: (0,) * len(shape))

    px = (length, STEP, width)
    grid_spec = pltpu.PrefetchScalarGridSpec(
        num_scalar_prefetch=2,
        grid=(pixels // STEP,),
        in_specs=[pl.BlockSpec(px, live_block), pl.BlockSpec(px, live_block), whole(absent.shape)]
        + [whole(item.shape) for item in weights],
        out_specs=[
            pl.BlockSpec(px, lambda i, c, m: (0, i, 0)),
            pl.BlockSpec(px, lambda i, c, m: (0, i, 0)),
            whole((chunks // 2, each, 128)),
            whole((chunks // 2, each, 128)),
        ],
        scratch_shapes=[
            pltpu.VMEM((count, 128, 384), F32),
            pltpu.VMEM((count, 128, 128), F32),
            pltpu.VMEM((count, 128, 512), F32),
            pltpu.VMEM((chunks * each, 128), F32),
            pltpu.VMEM((BLOCK, 112, 128), F32),
            pltpu.VMEM((BLOCK, 112, 128), F32),
            pltpu.VMEM((count, BLOCK, 112, 128), F32),
            pltpu.VMEM((count, BLOCK, 112, 128), F32),
            pltpu.VMEM((count, BLOCK, 112, 128), F32),
            pltpu.VMEM((count, BLOCK, 112, 128), F32),
            pltpu.VMEM((count, BLOCK, 112, 128), BF16),
            pltpu.VMEM((count, BLOCK, 112, 128), BF16),
            pltpu.VMEM((count, BLOCK, 128, 640), BF16),
            pltpu.VMEM((count, BLOCK, 112, 1024), BF16),
            pltpu.VMEM((count, BLOCK, 128, 128), BF16),
            pltpu.VMEM((count, BLOCK, 112, 512), BF16),
            pltpu.VMEM((count, BLOCK, 112, 512), BF16),
            pltpu.VMEM((BLOCK, 128, 128), BF16),
            pltpu.VMEM((BLOCK, 112, 128), BF16),
            pltpu.VMEM((BLOCK, 112, 512), BF16),
            pltpu.VMEM((BLOCK, 112, 384), BF16),
            pltpu.VMEM((count, BLOCK, HEADS, 128), F32),
            pltpu.VMEM((count, 512, 128), BF16),
            pltpu.VMEM((pixels, 128), F32),
            pltpu.VMEM((CHUNK, 3, 128, 128), BF16),
            pltpu.VMEM((count, 128, 512), F32),
            pltpu.VMEM((count, 6, 8, 128), F32),
            pltpu.VMEM((count, 8, 512), F32),
            pltpu.VMEM((length * STEP, 128), F32),
            pltpu.VMEM((length * STEP, 128), F32),
        ]
        + [pltpu.VMEM((112, 256), BF16)] * 16,
    )
    return pl.pallas_call(
        functools.partial(body, peers=peers, length=length),
        grid_spec=grid_spec,
        out_shape=[
            jax.ShapeDtypeStruct(tokens.shape, BF16),
            jax.ShapeDtypeStruct(tokens.shape, BF16),
            jax.ShapeDtypeStruct((chunks // 2, each, 128), BF16),
            jax.ShapeDtypeStruct((chunks // 2, each, 128), BF16),
        ],
        compiler_params=pltpu.CompilerParams(vmem_limit_bytes=56 << 20),
        name="layers",
    )(counts, me, tokens, cotangent, absent, *weights)


def local(tokens, absent, send_counts, *rest, sizes):
    weights, cotangent = rest[:-1], rest[-1]
    chunks = sizes[0] * sizes[1]
    each = (weights[0].shape[0] * PACK + 16 * chunks - 1) // (16 * chunks) * 16
    me = (lax.axis_index("tile") * sizes[1] + lax.axis_index("rep")).astype(jnp.int32).reshape(1)
    out, gtok, keep, send = layers(
        send_counts,
        me,
        tokens.transpose(1, 0, 2),
        cotangent.transpose(1, 0, 2),
        absent,
        weights,
        chunks,
        each,
    )
    own, other = reduce_all(keep, send, sizes)
    grads = unpack(me, own, other, weights)
    return (out.transpose(1, 0, 2), gtok.transpose(1, 0, 2)) + tuple(grads)


def solution(mesh):
    split = P(("tile", "rep"))
    sizes = (mesh.shape["tile"], mesh.shape["rep"])
    return jax.shard_map(
        functools.partial(local, sizes=sizes),
        mesh=mesh,
        in_specs=(split, split, split) + (P(),) * 11 + (split,),
        out_specs=(split, split) + (P(),) * 11,
        check_vma=False,
    )
```
